32 devices in a mesh: grp: 2 (over x), seq: 16 (over z, y, core).
Axes of the slice: x: 2, y: 2, z: 4, core: 2. Of those that a mesh axis runs over, the one named last changes fastest.
Arguments:
- tokens: bfloat16 [16384, 1024], P(('grp', 'seq')), may hold values from -20 to 20
- qkv_weight: bfloat16 [1024, 1536], replicated, may hold values from -2 to 2
- cov_embed: bfloat16 [64, 1024], P(('grp', 'seq')), may hold values from -20 to 20
- cov_slot: int32 [32], replicated, may hold values from 0 to 63, as said below
- block_links: int32 [128, 2], P(('grp', 'seq')), may hold values from 0 to 1, as said below
Outputs:
- attended: bfloat16 [16384, 512], P(('grp', 'seq'))
The draws below stay inside these ranges and needn't reach their ends.
Inputs may be any that keep to these rules, and one draw needn't show every extreme that they name: The values are distinct; covariate c is held in slot cov_slot[c], on the device that holds that row of cov_embed. block_links[b, 1] equals block_links[b + 1, 0]; block_links[0, 0] and block_links[127, 1] are 0.
All inputs are finite; a program needn't handle non-finite values.
Results may differ from the reference program's by a relative error of at most 0.0015.
The reference program's roundings to bfloat16 on the way count: a program that leaves them out, or rounds other values in their place, can miss the bound.
Values may be sent and summed in bfloat16 or wider, within the bound.
A program may use at most 64 MiB of HBM per device.

```python
import math
import jax
import jax.numpy as jnp
from jax import lax

D = 1024
HEADS = 8
HEAD_SIZE = 64
BLOCK = 128
TOK_DEV = 512
TOKENS = 16384
NBLOCKS = 128
SLOTS = 64
COV = 32


def lifted_rows(key, salt, count):
    rows = jnp.clip(jax.random.normal(jax.random.fold_in(key, salt), (count, D), jnp.float32), -6.0, 6.0)
    return rows


def draw_tokens(key, part):
    return lifted_rows(key, 11, TOKENS).astype(jnp.bfloat16)


def draw_cov_embed(key, part):
    return lifted_rows(key, 31, SLOTS).astype(jnp.bfloat16)


def draw_qkv_weight(key, part):
    attn_width = HEADS * HEAD_SIZE
    spread = 1.5 / math.sqrt(D)
    raw = jnp.clip(jax.random.normal(jax.random.fold_in(key, 201), (D, 3 * attn_width), jnp.float32), -4.0, 4.0)
    return (spread * raw).astype(jnp.bfloat16)


def draw_cov_slot(key, part):
    return jax.random.permutation(jax.random.fold_in(key, 301), SLOTS)[:COV].astype(jnp.int32)


def draw_block_links(key, part):
    starts = jax.random.randint(jax.random.fold_in(key, 401), (NBLOCKS,), 0, 4) == 0
    starts = starts.at[0].set(True)
    left_open = 1 - starts.astype(jnp.int32)
    right_open = jnp.concatenate([left_open[1:], jnp.zeros((1,), jnp.int32)])
    return jnp.stack([left_open, right_open], axis=1)


def setup_inputs(seed: int = 0) -> dict:
    key_of = jax.random.split(jax.random.key(seed), 6)
    return {
        "tokens": draw_tokens(jax.random.fold_in(key_of[5], 71), 0),
        "qkv_weight": draw_qkv_weight(jax.random.fold_in(key_of[5], 71), 0),
        "cov_embed": draw_cov_embed(jax.random.fold_in(key_of[5], 71), 0),
        "cov_slot": draw_cov_slot(jax.random.fold_in(key_of[5], 71), 0),
        "block_links": draw_block_links(jax.random.fold_in(key_of[5], 71), 0),
    }


masked_score = -1e+30

def window_attend(queries, before, middle, after, left_open, right_open, cov_kv, head_count):
    blocks, block_rows, attn_width = queries.shape
    head_width = attn_width // head_count
    score_scale = 1.0 / math.sqrt(head_width)
    query_heads = queries.reshape(blocks, block_rows, head_count, head_width)

    def divide_parts(joined):
        key_part = joined[:, :, :attn_width].reshape(blocks, block_rows, head_count, head_width)
        value_part = joined[:, :, attn_width:].reshape(blocks, block_rows, head_count, head_width)
        return (key_part, value_part)
    key_before, value_before = divide_parts(before)
    key_middle, value_middle = divide_parts(middle)
    key_after, value_after = divide_parts(after)
    cov_count = cov_kv.shape[0]
    cov_keys = cov_kv[:, :attn_width].reshape(cov_count, head_count, head_width)
    cov_values = cov_kv[:, attn_width:].reshape(cov_count, head_count, head_width)

    def local_scores(key_part):
        return jnp.einsum('nqhd,nkhd->nqhk', query_heads, key_part, preferred_element_type=jnp.float32) * score_scale
    score_before = jnp.where((left_open > 0)[:, None, None, None], local_scores(key_before), masked_score)
    score_middle = local_scores(key_middle)
    score_after = jnp.where((right_open > 0)[:, None, None, None], local_scores(key_after), masked_score)
    score_global = jnp.einsum('nqhd,chd->nqhc', query_heads, cov_keys, preferred_element_type=jnp.float32) * score_scale
    highest = jnp.maximum(jnp.maximum(lax.optimization_barrier(jnp.max(score_before, axis=-1, keepdims=True)), lax.optimization_barrier(jnp.max(score_middle, axis=-1, keepdims=True))), jnp.maximum(lax.optimization_barrier(jnp.max(score_after, axis=-1, keepdims=True)), lax.optimization_barrier(jnp.max(score_global, axis=-1, keepdims=True))))
    weight_before = jnp.exp(score_before - highest)
    weight_middle = jnp.exp(score_middle - highest)
    weight_after = jnp.exp(score_after - highest)
    weight_global = jnp.exp(score_global - highest)
    denominator = lax.optimization_barrier(jnp.sum(weight_before, axis=-1)) + lax.optimization_barrier(jnp.sum(weight_middle, axis=-1)) + lax.optimization_barrier(jnp.sum(weight_after, axis=-1)) + lax.optimization_barrier(jnp.sum(weight_global, axis=-1))

    def local_values(weights, value_part):
        return jnp.einsum('nqhk,nkhd->nqhd', weights.astype(jnp.bfloat16), value_part, preferred_element_type=jnp.float32)
    summed = local_values(weight_before, value_before) + local_values(weight_middle, value_middle)
    summed = summed + local_values(weight_after, value_after)
    summed = summed + jnp.einsum('nqhc,chd->nqhd', weight_global.astype(jnp.bfloat16), cov_values, preferred_element_type=jnp.float32)
    result = (summed / denominator[..., None]).astype(jnp.bfloat16)
    return result.reshape(blocks * block_rows, attn_width)

def reference(tokens, qkv_weight, cov_embed, cov_slot, block_links):
    attn_width = HEADS * HEAD_SIZE
    shards = TOKENS // TOK_DEV
    blocks = TOK_DEV // BLOCK

    def project(rows):
        return jnp.dot(rows, qkv_weight, preferred_element_type=jnp.float32).astype(jnp.bfloat16)
    projected = lax.map(project, tokens.reshape(shards, TOK_DEV, D)).reshape(TOKENS, 3 * attn_width)
    queries = projected[:, :attn_width]
    keyvalue = projected[:, attn_width:]
    zeros_rim = jnp.zeros((BLOCK, 2 * attn_width), keyvalue.dtype)
    padded = jnp.concatenate([zeros_rim, keyvalue, zeros_rim], axis=0)
    chosen = jnp.take(cov_embed, cov_slot.astype(jnp.int32), axis=0)
    cov_kv = jnp.dot(chosen, qkv_weight[:, attn_width:], preferred_element_type=jnp.float32).astype(jnp.bfloat16)

    def one_shard(index):
        start = (index * TOK_DEV).astype(jnp.int32)
        rows = lax.dynamic_slice_in_dim(queries, start, TOK_DEV, 0).reshape(blocks, BLOCK, attn_width)
        before = lax.dynamic_slice_in_dim(padded, start, TOK_DEV, 0).reshape(blocks, BLOCK, 2 * attn_width)
        middle = lax.dynamic_slice_in_dim(padded, start + BLOCK, TOK_DEV, 0).reshape(blocks, BLOCK, 2 * attn_width)
        after = lax.dynamic_slice_in_dim(padded, start + 2 * BLOCK, TOK_DEV, 0).reshape(blocks, BLOCK, 2 * attn_width)
        edges = lax.dynamic_slice_in_dim(block_links, (index * blocks).astype(jnp.int32), blocks, 0)
        return window_attend(rows, before, middle, after, edges[:, 0], edges[:, 1], cov_kv, HEADS)
    result = lax.map(one_shard, jnp.arange(shards, dtype=jnp.int32))
    return result.reshape(TOKENS, attn_width)
```

```python
import functools
import math

import jax
import jax.numpy as jnp
from jax import lax
from jax.experimental import pallas as pl
from jax.experimental.pallas import tpu as pltpu
from jax.sharding import PartitionSpec as P

HEADS = 8
BLOCK = 128
LANES = 128
NT = (((1,), (1,)), ((), ()))
NN = (((1,), (0,)), ((), ()))
F32 = jnp.float32
BF16 = jnp.bfloat16
CLOSED = 1e30


def dot(a, b, dims=NN):
    return lax.dot_general(a, b, dims, preferred_element_type=F32)


def kernel(
    grid_shape,
    slot_ref,
    links_ref,
    x_hbm,
    w_hbm,
    cov_ref,
    out_ref,
    x,
    w,
    q,
    keys,
    values,
    cov_tmp,
    cov_mine,
    cov_all,
    cov_sum,
    load_sem,
    cov_send,
    cov_recv,
    halo_send,
    halo_recv,
):
    groups, seqs = grid_shape
    count = groups * seqs
    rows, depth = x.shape
    attn = q.shape[1]
    blocks = rows // BLOCK
    slots_dev = cov_ref.shape[0]
    pieces = depth // LANES
    tile_rows = slots_dev * pieces
    chosen_rows = slot_ref.shape[1]
    me = lax.axis_index("grp") * seqs + lax.axis_index("seq")

    def place(index):
        return (index // seqs, index % seqs)

    chunk = attn // 2
    order = [2, 3, 4, 5, 0, 1]
    loads = []
    x_load = pltpu.make_async_copy(x_hbm, x, load_sem.at[6])
    x_load.start()
    for i, c in enumerate(order):
        part = pl.ds(c * chunk, chunk)
        cp = pltpu.make_async_copy(w_hbm.at[:, part], w.at[:, part], load_sem.at[i])
        cp.start()
        loads.append(cp)

    barrier = pltpu.get_barrier_semaphore()

    @pl.loop(1, count)
    def _(step):
        pl.semaphore_signal(
            barrier,
            inc=1,
            device_id=place(lax.rem(me + step, count)),
            device_id_type=pl.DeviceIdType.MESH,
        )

    cov_value = cov_ref[...].astype(F32)
    for j in range(pieces):
        cov_tmp[j * slots_dev : (j + 1) * slots_dev, :] = cov_value[:, j * LANES : (j + 1) * LANES]
    cov_mine[...] = cov_tmp[...].astype(BF16)
    cov_all[me] = cov_mine[...]
    pl.semaphore_wait(barrier, count - 1)

    @pl.loop(1, count)
    def _(step):
        pltpu.make_async_remote_copy(
            src_ref=cov_mine,
            dst_ref=cov_all.at[me],
            send_sem=cov_send,
            recv_sem=cov_recv,
            device_id=place(lax.rem(me + step, count)),
            device_id_type=pl.DeviceIdType.MESH,
        ).start()

    x_load.wait()
    for i in range(4):
        loads[i].wait()
        c = order[i]
        part = dot(x[...], w[:, c * chunk : (c + 1) * chunk]).astype(BF16)
        if i < 2:
            keys[BLOCK : BLOCK + rows, i * chunk : (i + 1) * chunk] = part
        else:
            k = i - 2
            for b in range(blocks):
                values[b + 1, k * chunk : (k + 1) * chunk, :] = part[
                    b * BLOCK : (b + 1) * BLOCK, :
                ].T

    def key_rows(b):
        return keys.at[pl.ds(b * BLOCK, BLOCK)]

    def edge_copies(source, target, peer, at):
        return [
            pltpu.make_async_remote_copy(
                src_ref=src,
                dst_ref=dst,
                send_sem=halo_send.at[at + n],
                recv_sem=halo_recv.at[at + n],
                device_id=place(peer),
                device_id_type=pl.DeviceIdType.MESH,
            )
            for n, (src, dst) in enumerate(
                [
                    (key_rows(source), key_rows(target)),
                    (values.at[source], values.at[target]),
                ]
            )
        ]

    to_left = edge_copies(1, blocks + 1, lax.max(me - 1, 0), 0)
    to_right = edge_copies(blocks, 0, lax.min(me + 1, count - 1), 2)
    has_left = me > 0
    has_right = me < count - 1

    @pl.when(has_left)
    def _():
        for cp in to_left:
            cp.start()

    @pl.when(has_right)
    def _():
        for cp in to_right:
            cp.start()

    @pl.when(me == 0)
    def _():
        keys[0:BLOCK, :] = jnp.zeros((BLOCK, attn), BF16)
        values[0] = jnp.zeros((attn, BLOCK), BF16)

    @pl.when(me == count - 1)
    def _():
        keys[BLOCK + rows : 2 * BLOCK + rows, :] = jnp.zeros((BLOCK, attn), BF16)
        values[blocks + 1] = jnp.zeros((attn, BLOCK), BF16)

    for i in (4, 5):
        loads[i].wait()
        c = order[i]
        part = dot(x[...], w[:, c * chunk : (c + 1) * chunk]).astype(BF16)
        q[:, c * chunk : (c + 1) * chunk] = part

    others = cov_all.at[pl.ds(0, count - 1)]
    pltpu.make_async_copy(others, others, cov_recv).wait()
    span = 32 if count % 32 == 0 else count
    cov_sum[...] = jnp.zeros_like(cov_sum)

    @pl.loop(0, count // span)
    def _(t):
        held = cov_all[pl.ds(t * span, span)].reshape(span * tile_rows, LANES)
        slot = slot_ref[...]
        base = (slot // slots_dev - t * span) * tile_rows + slot % slots_dev
        row = lax.broadcasted_iota(jnp.int32, (span * tile_rows, chosen_rows), 0)
        for j in range(pieces):
            pick = jnp.where(row == base + j * slots_dev, 1.0, 0.0).astype(BF16)
            cov_sum[:, j * LANES : (j + 1) * LANES] += lax.dot_general(
                pick, held, (((0,), (0,)), ((), ())), preferred_element_type=F32
            )

    chosen = cov_sum[...].astype(BF16)
    cov_keys = dot(chosen, w[:, attn : 2 * attn]).astype(BF16)
    cov_values = dot(chosen, w[:, 2 * attn :]).astype(BF16).T

    factor = math.log2(math.e) / math.sqrt(attn // HEADS)
    lane = lax.broadcasted_iota(jnp.int32, (BLOCK, LANES), 1)
    low = lane < LANES // 2

    def attend(b, p):
        cols = slice(p * LANES, (p + 1) * LANES)
        qp = q[b * BLOCK : (b + 1) * BLOCK, cols]
        zero = jnp.zeros_like(qp)
        both = jnp.concatenate([jnp.where(low, qp, zero), jnp.where(low, zero, qp)], axis=0)
        scores = dot(keys[b * BLOCK : (b + 3) * BLOCK, cols], both, NT)
        score_cov = dot(cov_keys[:, cols], both, NT)
        before, middle, after = (scores[i * BLOCK : (i + 1) * BLOCK] for i in range(3))
        open_before = links_ref[b, 0] > 0
        open_after = links_ref[b, 1] > 0

        def top(s):
            return jnp.max(s, axis=0, keepdims=True)

        highest = jnp.maximum(
            jnp.maximum(top(middle), top(score_cov)),
            jnp.maximum(
                jnp.where(open_before, top(before), -CLOSED),
                jnp.where(open_after, top(after), -CLOSED),
            ),
        )
        weights = [
            jnp.exp2((before - jnp.where(open_before, highest, CLOSED)) * factor),
            jnp.exp2((middle - highest) * factor),
            jnp.exp2((after - jnp.where(open_after, highest, CLOSED)) * factor),
            jnp.exp2((score_cov - highest) * factor),
        ]
        total = sum(jnp.sum(a, axis=0, keepdims=True) for a in weights)
        rounded = jnp.concatenate([a.astype(BF16) for a in weights], axis=0)
        value = jnp.concatenate(
            [values[b, cols], values[b + 1, cols], values[b + 2, cols], cov_values[cols, :]],
            axis=1,
        )
        summed = dot(value, rounded) * (1.0 / total)
        half = LANES // 2
        pair = jnp.concatenate([summed[:half, :BLOCK], summed[half:, BLOCK:]], axis=0)
        out_ref[b * BLOCK : (b + 1) * BLOCK, cols] = pair.T.astype(BF16)

    for b in range(1, blocks - 1):
        for p in range(attn // LANES):
            attend(b, p)

    @pl.when(has_left)
    def _():
        for cp in to_right:
            cp.wait_recv()

    @pl.when(has_right)
    def _():
        for cp in to_left:
            cp.wait_recv()

    for b in (0, blocks - 1):
        for p in range(attn // LANES):
            attend(b, p)

    @pl.when(has_left)
    def _():
        for cp in to_left:
            cp.wait_send()

    @pl.when(has_right)
    def _():
        for cp in to_right:
            cp.wait_send()

    pltpu.make_async_copy(others, others, cov_send).wait()


def local(grid_shape, tokens, qkv_weight, cov_embed, cov_slot, block_links):
    count = grid_shape[0] * grid_shape[1]
    rows, depth = tokens.shape
    attn = qkv_weight.shape[1] // 3
    blocks = rows // BLOCK
    tile_rows = cov_embed.shape[0] * depth // LANES
    cov = cov_slot.shape[0]
    vmem = pl.BlockSpec(memory_space=pltpu.VMEM)
    smem = pl.BlockSpec(memory_space=pltpu.SMEM)
    hbm = pl.BlockSpec(memory_space=pl.ANY)
    return pl.pallas_call(
        functools.partial(kernel, grid_shape),
        out_shape=jax.ShapeDtypeStruct((rows, attn), BF16),
        in_specs=[vmem, smem, hbm, hbm, vmem],
        out_specs=vmem,
        scratch_shapes=[
            pltpu.VMEM((rows, depth), BF16),
            pltpu.VMEM((depth, 3 * attn), BF16),
            pltpu.VMEM((rows, attn), BF16),
            pltpu.VMEM((rows + 2 * BLOCK, attn), BF16),
            pltpu.VMEM((blocks + 2, attn, BLOCK), BF16),
            pltpu.VMEM((tile_rows, LANES), F32),
            pltpu.VMEM((tile_rows, LANES), BF16),
            pltpu.VMEM((count, tile_rows, LANES), BF16),
            pltpu.VMEM((cov, depth), F32),
            pltpu.SemaphoreType.DMA((7,)),
            pltpu.SemaphoreType.DMA,
            pltpu.SemaphoreType.DMA,
            pltpu.SemaphoreType.DMA((4,)),
            pltpu.SemaphoreType.DMA((4,)),
        ],
        compiler_params=pltpu.CompilerParams(
            collective_id=0, has_side_effects=True, vmem_limit_bytes=56 * 1024 * 1024
        ),
        cost_estimate=pl.CostEstimate(
            flops=2 * rows * depth * 3 * attn, bytes_accessed=5 << 20, transcendentals=rows * 4096
        ),
    )(cov_slot.reshape(1, cov), block_links, tokens, qkv_weight, cov_embed)


def solution(mesh):
    placed = (P(("grp", "seq"), None), P(), P(("grp", "seq"), None), P(), P(("grp", "seq"), None))
    grid_shape = (mesh.shape["grp"], mesh.shape["seq"])
    return jax.shard_map(
        functools.partial(local, grid_shape),
        mesh=mesh,
        in_specs=placed,
        out_specs=P(("grp", "seq"), None),
        check_vma=False,
    )
```

```python
import functools
import math

import jax
import jax.numpy as jnp
from jax import lax
from jax.experimental import pallas as pl
from jax.experimental.pallas import tpu as pltpu
from jax.sharding import PartitionSpec as P

HEADS = 8
BLOCK = 128
LANES = 128
NT = (((1,), (1,)), ((), ()))
NN = (((1,), (0,)), ((), ()))
F32 = jnp.float32
BF16 = jnp.bfloat16
CLOSED = 1e30
INNER = 4


def dot(a, b, dims=NN):
    return lax.dot_general(a, b, dims, preferred_element_type=F32)


def kernel(
    grid_shape,
    slot_ref,
    links_ref,
    x_hbm,
    w_hbm,
    cov_ref,
    out_ref,
    x,
    w,
    q,
    keys,
    values,
    cov_tmp,
    cov_mine,
    cov_all,
    cov_sum,
    halo,
    load_sem,
    line_send,
    line_recv,
    plane_send,
    plane_recv,
    halo_send,
    halo_recv,
):
    groups, seqs = grid_shape
    count = groups * seqs
    rows, depth = x.shape
    attn = q.shape[1]
    blocks = rows // BLOCK
    slots_dev = cov_ref.shape[0]
    pieces = depth // LANES
    tile_rows = slots_dev * pieces
    chosen_rows = slot_ref.shape[1]
    me = lax.axis_index("grp") * seqs + lax.axis_index("seq")

    def place(index):
        return (index // seqs, index % seqs)

    inner = INNER if seqs % INNER == 0 else 1
    length = seqs // inner
    width = groups * inner
    seq = lax.axis_index("seq")
    at_line = seq // inner
    at_plane = lax.axis_index("grp") * inner + seq % inner

    def on_line(step):
        return (lax.axis_index("grp"), lax.rem(at_line + step, length) * inner + seq % inner)

    def on_plane(step):
        other = lax.rem(at_plane + step, width)
        return (other // inner, at_line * inner + other % inner)

    left = place(lax.max(me - 1, 0))
    right = place(lax.min(me + 1, count - 1))
    has_left = me > 0
    has_right = me < count - 1
    mesh_id = pl.DeviceIdType.MESH
    barrier = pltpu.get_barrier_semaphore()

    def greet(device):
        pl.semaphore_signal(barrier, inc=1, device_id=device, device_id_type=mesh_id)

    pl.when(has_left)(lambda: greet(left))
    pl.when(has_right)(lambda: greet(right))
    pl.loop(1, length)(lambda step: greet(on_line(step)))
    pl.loop(1, width)(lambda step: greet(on_plane(step)))

    loads = [pltpu.make_async_copy(x_hbm, x, load_sem.at[0])]
    parts = 4
    step_rows = depth // parts
    for i in range(parts):
        part = pl.ds(i * step_rows, step_rows)
        loads.append(pltpu.make_async_copy(w_hbm.at[part], w.at[part], load_sem.at[i + 1]))
    for cp in loads:
        cp.start()

    cov_value = cov_ref[...].astype(F32)
    for j in range(pieces):
        cov_tmp[j * slots_dev : (j + 1) * slots_dev, :] = cov_value[:, j * LANES : (j + 1) * LANES]
    cov_mine[...] = cov_tmp[...].astype(BF16)
    cov_all[at_plane, at_line] = cov_mine[...]

    @pl.when(me == 0)
    def _():
        halo[0] = jnp.zeros((BLOCK, depth), BF16)

    @pl.when(me == count - 1)
    def _():
        halo[1] = jnp.zeros((BLOCK, depth), BF16)

    pl.semaphore_wait(
        barrier, length + width - 2 + has_left.astype(jnp.int32) + has_right.astype(jnp.int32)
    )

    @pl.loop(1, length)
    def _(step):
        pltpu.make_async_remote_copy(
            src_ref=cov_mine,
            dst_ref=cov_all.at[at_plane, at_line],
            send_sem=line_send,
            recv_sem=line_recv,
            device_id=on_line(step),
            device_id_type=mesh_id,
        ).start()

    def edge(first, side, device):
        return pltpu.make_async_remote_copy(
            src_ref=x_hbm.at[pl.ds(first, BLOCK)],
            dst_ref=halo.at[side],
            send_sem=halo_send.at[side],
            recv_sem=halo_recv.at[side],
            device_id=device,
            device_id_type=mesh_id,
        )

    to_left = edge(0, 1, left)
    to_right = edge(rows - BLOCK, 0, right)
    pl.when(has_left)(to_left.start)
    pl.when(has_right)(to_right.start)

    if length > 1:
        others = cov_all.at[0, pl.ds(0, length - 1)]
        pltpu.make_async_copy(others, others, line_recv).wait()

    @pl.loop(1, width)
    def _(step):
        pltpu.make_async_remote_copy(
            src_ref=cov_all.at[at_plane],
            dst_ref=cov_all.at[at_plane],
            send_sem=plane_send,
            recv_sem=plane_recv,
            device_id=on_plane(step),
            device_id_type=mesh_id,
        ).start()

    for cp in loads:
        cp.wait()
    part = dot(x[...], w[:, attn:]).astype(BF16)
    keys[BLOCK : BLOCK + rows, :] = part[:, :attn]
    for b in range(blocks):
        values[b + 1] = part[b * BLOCK : (b + 1) * BLOCK, attn:].T
    q[...] = dot(x[...], w[:, :attn]).astype(BF16)

    planes = cov_all.at[pl.ds(0, width - 1)]
    pltpu.make_async_copy(planes, planes, plane_recv).wait()
    span = max(1, 32 // length)
    span = span if width % span == 0 else 1
    span_rows = span * length * tile_rows
    cov_sum[...] = jnp.zeros_like(cov_sum)

    @pl.loop(0, width // span)
    def _(t):
        held = cov_all[pl.ds(t * span, span)].reshape(span_rows, LANES)
        slot = slot_ref[...]
        device = slot // slots_dev
        where_seq = device % seqs
        plane = (device // seqs) * inner + where_seq % inner
        tile = (plane - t * span) * length + where_seq // inner
        base = tile * tile_rows + slot % slots_dev
        row = lax.broadcasted_iota(jnp.int32, (span_rows, chosen_rows), 0)
        for j in range(pieces):
            pick = jnp.where(row == base + j * slots_dev, 1.0, 0.0).astype(BF16)
            cov_sum[:, j * LANES : (j + 1) * LANES] += lax.dot_general(
                pick, held, (((0,), (0,)), ((), ())), preferred_element_type=F32
            )

    cov_kv = dot(cov_sum[...].astype(BF16), w[:, attn:]).astype(BF16)
    cov_keys = cov_kv[:, :attn]
    cov_values = cov_kv[:, attn:].T

    factor = math.log2(math.e) / math.sqrt(attn // HEADS)
    lane = lax.broadcasted_iota(jnp.int32, (BLOCK, LANES), 1)
    low = lane < LANES // 2

    def attend(b, p):
        cols = slice(p * LANES, (p + 1) * LANES)
        qp = q[b * BLOCK : (b + 1) * BLOCK, cols]
        zero = jnp.zeros_like(qp)
        both = jnp.concatenate([jnp.where(low, qp, zero), jnp.where(low, zero, qp)], axis=0)
        scores = dot(keys[b * BLOCK : (b + 3) * BLOCK, cols], both, NT)
        score_cov = dot(cov_keys[:, cols], both, NT)
        before, middle, after = (scores[i * BLOCK : (i + 1) * BLOCK] for i in range(3))
        open_before = links_ref[0, b] > 0
        open_after = links_ref[1, b] > 0

        def top(s):
            return jnp.max(s, axis=0, keepdims=True)

        highest = jnp.maximum(
            jnp.maximum(top(middle), top(score_cov)),
            jnp.maximum(
                jnp.where(open_before, top(before), -CLOSED),
                jnp.where(open_after, top(after), -CLOSED),
            ),
        )
        weights = [
            jnp.exp2((before - jnp.where(open_before, highest, CLOSED)) * factor),
            jnp.exp2((middle - highest) * factor),
            jnp.exp2((after - jnp.where(open_after, highest, CLOSED)) * factor),
            jnp.exp2((score_cov - highest) * factor),
        ]
        total = sum(jnp.sum(a, axis=0, keepdims=True) for a in weights)
        rounded = jnp.concatenate([a.astype(BF16) for a in weights], axis=0)
        value = jnp.concatenate(
            [values[b, cols], values[b + 1, cols], values[b + 2, cols], cov_values[cols, :]],
            axis=1,
        )
        summed = dot(value, rounded) * (1.0 / total)
        half = LANES // 2
        pair = jnp.concatenate([summed[:half, :BLOCK], summed[half:, BLOCK:]], axis=0)
        out_ref[b * BLOCK : (b + 1) * BLOCK, cols] = pair.T.astype(BF16)

    for b in range(1, blocks - 1):
        for p in range(attn // LANES):
            attend(b, p)

    pl.when(has_left)(to_right.wait_recv)
    pl.when(has_right)(to_left.wait_recv)
    part = dot(halo[...].reshape(2 * BLOCK, depth), w[:, attn:]).astype(BF16)
    keys[0:BLOCK, :] = part[:BLOCK, :attn]
    keys[BLOCK + rows : 2 * BLOCK + rows, :] = part[BLOCK:, :attn]
    values[0] = part[:BLOCK, attn:].T
    values[blocks + 1] = part[BLOCK:, attn:].T

    for b in (0, blocks - 1):
        for p in range(attn // LANES):
            attend(b, p)

    pl.when(has_left)(to_left.wait_send)
    pl.when(has_right)(to_right.wait_send)
    if length > 1:
        pltpu.make_async_copy(others, others, line_send).wait()
    pltpu.make_async_copy(planes, planes, plane_send).wait()


def local(grid_shape, tokens, qkv_weight, cov_embed, cov_slot, block_links):
    count = grid_shape[0] * grid_shape[1]
    rows, depth = tokens.shape
    attn = qkv_weight.shape[1] // 3
    blocks = rows // BLOCK
    tile_rows = cov_embed.shape[0] * depth // LANES
    cov = cov_slot.shape[0]
    width = grid_shape[0] * (INNER if grid_shape[1] % INNER == 0 else 1)
    vmem = pl.BlockSpec(memory_space=pltpu.VMEM)
    smem = pl.BlockSpec(memory_space=pltpu.SMEM)
    hbm = pl.BlockSpec(memory_space=pl.ANY)
    return pl.pallas_call(
        functools.partial(kernel, grid_shape),
        out_shape=pltpu.VMEM((rows, attn), BF16),
        in_specs=[vmem, smem, hbm, hbm, vmem],
        out_specs=vmem,
        scratch_shapes=[
            pltpu.VMEM((rows, depth), BF16),
            pltpu.VMEM((depth, 3 * attn), BF16),
            pltpu.VMEM((rows, attn), BF16),
            pltpu.VMEM((rows + 2 * BLOCK, attn), BF16),
            pltpu.VMEM((blocks + 2, attn, BLOCK), BF16),
            pltpu.VMEM((tile_rows, LANES), F32),
            pltpu.VMEM((tile_rows, LANES), BF16),
            pltpu.VMEM((width, count // width, tile_rows, LANES), BF16),
            pltpu.VMEM((cov, depth), F32),
            pltpu.VMEM((2, BLOCK, depth), BF16),
            pltpu.SemaphoreType.DMA((5,)),
            pltpu.SemaphoreType.DMA,
            pltpu.SemaphoreType.DMA,
            pltpu.SemaphoreType.DMA,
            pltpu.SemaphoreType.DMA,
            pltpu.SemaphoreType.DMA((2,)),
            pltpu.SemaphoreType.DMA((2,)),
        ],
        compiler_params=pltpu.CompilerParams(
            collective_id=0, has_side_effects=True, vmem_limit_bytes=56 * 1024 * 1024
        ),
        cost_estimate=pl.CostEstimate(
            flops=2 * rows * depth * 3 * attn, bytes_accessed=5 << 20, transcendentals=rows * 4096
        ),
    )(cov_slot.reshape(1, cov), block_links.T, tokens, qkv_weight, cov_embed)


def solution(mesh):
    placed = (P(("grp", "seq"), None), P(), P(("grp", "seq"), None), P(), P(("grp", "seq"), None))
    grid_shape = (mesh.shape["grp"], mesh.shape["seq"])
    return jax.shard_map(
        functools.partial(local, grid_shape),
        mesh=mesh,
        in_specs=placed,
        out_specs=P(("grp", "seq"), None),
        check_vma=False,
    )
```

```python
import functools
import math

import jax
import jax.numpy as jnp
from jax import lax
from jax.experimental import pallas as pl
from jax.experimental.pallas import tpu as pltpu
from jax.sharding import PartitionSpec as P

HEADS = 8
BLOCK = 128
LANES = 128
NT = (((1,), (1,)), ((), ()))
NN = (((1,), (0,)), ((), ()))
F32 = jnp.float32
BF16 = jnp.bfloat16
CLOSED = 1e30


def dot(a, b, dims=NN):
    return lax.dot_general(a, b, dims, preferred_element_type=F32)


def kernel(
    grid_shape,
    slot_ref,
    links_ref,
    x_hbm,
    w_hbm,
    cov_ref,
    out_ref,
    x,
    w,
    q,
    keys,
    values,
    cov_tmp,
    cov_mine,
    cov_all,
    cov_sum,
    load_sem,
    cov_send,
    cov_recv,
    halo_send,
    halo_recv,
):
    groups, seqs = grid_shape
    count = groups * seqs
    rows, depth = x.shape
    attn = q.shape[1]
    blocks = rows // BLOCK
    slots_dev = cov_ref.shape[0]
    pieces = depth // LANES
    tile_rows = slots_dev * pieces
    chosen_rows = slot_ref.shape[1]
    me = lax.axis_index("grp") * seqs + lax.axis_index("seq")

    def place(index):
        return (index // seqs, index % seqs)

    chunk = attn // 2
    order = [2, 3, 4, 5, 0, 1]
    loads = []
    x_load = pltpu.make_async_copy(x_hbm, x, load_sem.at[6])
    x_load.start()
    for i, c in enumerate(order):
        part = pl.ds(c * chunk, chunk)
        cp = pltpu.make_async_copy(w_hbm.at[:, part], w.at[:, part], load_sem.at[i])
        cp.start()
        loads.append(cp)

    barrier = pltpu.get_barrier_semaphore()

    @pl.loop(1, count)
    def _(step):
        pl.semaphore_signal(
            barrier,
            inc=1,
            device_id=place(lax.rem(me + step, count)),
            device_id_type=pl.DeviceIdType.MESH,
        )

    cov_value = cov_ref[...].astype(F32)
    for j in range(pieces):
        cov_tmp[j * slots_dev : (j + 1) * slots_dev, :] = cov_value[:, j * LANES : (j + 1) * LANES]
    cov_mine[...] = cov_tmp[...].astype(BF16)
    cov_all[me] = cov_mine[...]
    pl.semaphore_wait(barrier, count - 1)

    @pl.loop(1, count)
    def _(step):
        pltpu.make_async_remote_copy(
            src_ref=cov_mine,
            dst_ref=cov_all.at[me],
            send_sem=cov_send,
            recv_sem=cov_recv,
            device_id=place(lax.rem(me + step, count)),
            device_id_type=pl.DeviceIdType.MESH,
        ).start()

    x_load.wait()
    for i in range(4):
        loads[i].wait()
        c = order[i]
        part = dot(x[...], w[:, c * chunk : (c + 1) * chunk]).astype(BF16)
        if i < 2:
            keys[BLOCK : BLOCK + rows, i * chunk : (i + 1) * chunk] = part
        else:
            k = i - 2
            for b in range(blocks):
                values[b + 1, k * chunk : (k + 1) * chunk, :] = part[
                    b * BLOCK : (b + 1) * BLOCK, :
                ].T

    def key_rows(b):
        return keys.at[pl.ds(b * BLOCK, BLOCK)]

    def edge_copies(source, target, peer, at):
        return [
            pltpu.make_async_remote_copy(
                src_ref=src,
                dst_ref=dst,
                send_sem=halo_send.at[at + n],
                recv_sem=halo_recv.at[at + n],
                device_id=place(peer),
                device_id_type=pl.DeviceIdType.MESH,
            )
            for n, (src, dst) in enumerate(
                [
                    (key_rows(source), key_rows(target)),
                    (values.at[source], values.at[target]),
                ]
            )
        ]

    to_left = edge_copies(1, blocks + 1, lax.max(me - 1, 0), 0)
    to_right = edge_copies(blocks, 0, lax.min(me + 1, count - 1), 2)
    has_left = me > 0
    has_right = me < count - 1

    @pl.when(has_left)
    def _():
        for cp in to_left:
            cp.start()

    @pl.when(has_right)
    def _():
        for cp in to_right:
            cp.start()

    @pl.when(me == 0)
    def _():
        keys[0:BLOCK, :] = jnp.zeros((BLOCK, attn), BF16)
        values[0] = jnp.zeros((attn, BLOCK), BF16)

    @pl.when(me == count - 1)
    def _():
        keys[BLOCK + rows : 2 * BLOCK + rows, :] = jnp.zeros((BLOCK, attn), BF16)
        values[blocks + 1] = jnp.zeros((attn, BLOCK), BF16)

    for i in (4, 5):
        loads[i].wait()
        c = order[i]
        part = dot(x[...], w[:, c * chunk : (c + 1) * chunk]).astype(BF16)
        q[:, c * chunk : (c + 1) * chunk] = part

    others = cov_all.at[pl.ds(0, count - 1)]
    pltpu.make_async_copy(others, others, cov_recv).wait()
    span = 32 if count % 32 == 0 else count
    cov_sum[...] = jnp.zeros_like(cov_sum)

    @pl.loop(0, count // span)
    def _(t):
        held = cov_all[pl.ds(t * span, span)].reshape(span * tile_rows, LANES)
        slot = slot_ref[...]
        base = (slot // slots_dev - t * span) * tile_rows + slot % slots_dev
        row = lax.broadcasted_iota(jnp.int32, (span * tile_rows, chosen_rows), 0)
        for j in range(pieces):
            pick = jnp.where(row == base + j * slots_dev, 1.0, 0.0).astype(BF16)
            cov_sum[:, j * LANES : (j + 1) * LANES] += lax.dot_general(
                pick, held, (((0,), (0,)), ((), ())), preferred_element_type=F32
            )

    chosen = cov_sum[...].astype(BF16)
    cov_keys = dot(chosen, w[:, attn : 2 * attn]).astype(BF16)
    cov_values = dot(chosen, w[:, 2 * attn :]).astype(BF16).T

    factor = math.log2(math.e) / math.sqrt(attn // HEADS)
    lane = lax.broadcasted_iota(jnp.int32, (BLOCK, LANES), 1)
    low = lane < LANES // 2

    def attend(b, p):
        cols = slice(p * LANES, (p + 1) * LANES)
        qp = q[b * BLOCK : (b + 1) * BLOCK, cols]
        zero = jnp.zeros_like(qp)
        both = jnp.concatenate([jnp.where(low, qp, zero), jnp.where(low, zero, qp)], axis=0)
        scores = dot(keys[b * BLOCK : (b + 3) * BLOCK, cols], both, NT)
        score_cov = dot(cov_keys[:, cols], both, NT)
        before, middle, after = (scores[i * BLOCK : (i + 1) * BLOCK] for i in range(3))
        open_before = links_ref[0, b] > 0
        open_after = links_ref[1, b] > 0

        def top(s):
            return jnp.max(s, axis=0, keepdims=True)

        highest = jnp.maximum(
            jnp.maximum(top(middle), top(score_cov)),
            jnp.maximum(
                jnp.where(open_before, top(before), -CLOSED),
                jnp.where(open_after, top(after), -CLOSED),
            ),
        )
        weights = [
            jnp.exp2((before - jnp.where(open_before, highest, CLOSED)) * factor),
            jnp.exp2((middle - highest) * factor),
            jnp.exp2((after - jnp.where(open_after, highest, CLOSED)) * factor),
            jnp.exp2((score_cov - highest) * factor),
        ]
        total = sum(jnp.sum(a, axis=0, keepdims=True) for a in weights)
        rounded = jnp.concatenate([a.astype(BF16) for a in weights], axis=0)
        value = jnp.concatenate(
            [values[b, cols], values[b + 1, cols], values[b + 2, cols], cov_values[cols, :]],
            axis=1,
        )
        summed = dot(value, rounded) * (1.0 / total)
        half = LANES // 2
        pair = jnp.concatenate([summed[:half, :BLOCK], summed[half:, BLOCK:]], axis=0)
        out_ref[b * BLOCK : (b + 1) * BLOCK, cols] = pair.T.astype(BF16)

    for b in range(1, blocks - 1):
        for p in range(attn // LANES):
            attend(b, p)

    @pl.when(has_left)
    def _():
        for cp in to_right:
            cp.wait_recv()

    @pl.when(has_right)
    def _():
        for cp in to_left:
            cp.wait_recv()

    for b in (0, blocks - 1):
        for p in range(attn // LANES):
            attend(b, p)

    @pl.when(has_left)
    def _():
        for cp in to_left:
            cp.wait_send()

    @pl.when(has_right)
    def _():
        for cp in to_right:
            cp.wait_send()

    pltpu.make_async_copy(others, others, cov_send).wait()


def local(grid_shape, tokens, qkv_weight, cov_embed, cov_slot, block_links):
    count = grid_shape[0] * grid_shape[1]
    rows, depth = tokens.shape
    attn = qkv_weight.shape[1] // 3
    blocks = rows // BLOCK
    tile_rows = cov_embed.shape[0] * depth // LANES
    cov = cov_slot.shape[0]
    vmem = pl.BlockSpec(memory_space=pltpu.VMEM)
    smem = pl.BlockSpec(memory_space=pltpu.SMEM)
    hbm = pl.BlockSpec(memory_space=pl.ANY)
    return pl.pallas_call(
        functools.partial(kernel, grid_shape),
        out_shape=pltpu.VMEM((rows, attn), BF16),
        in_specs=[vmem, smem, hbm, hbm, vmem],
        out_specs=vmem,
        scratch_shapes=[
            pltpu.VMEM((rows, depth), BF16),
            pltpu.VMEM((depth, 3 * attn), BF16),
            pltpu.VMEM((rows, attn), BF16),
            pltpu.VMEM((rows + 2 * BLOCK, attn), BF16),
            pltpu.VMEM((blocks + 2, attn, BLOCK), BF16),
            pltpu.VMEM((tile_rows, LANES), F32),
            pltpu.VMEM((tile_rows, LANES), BF16),
            pltpu.VMEM((count, tile_rows, LANES), BF16),
            pltpu.VMEM((cov, depth), F32),
            pltpu.SemaphoreType.DMA((7,)),
            pltpu.SemaphoreType.DMA,
            pltpu.SemaphoreType.DMA,
            pltpu.SemaphoreType.DMA((4,)),
            pltpu.SemaphoreType.DMA((4,)),
        ],
        compiler_params=pltpu.CompilerParams(
            collective_id=0, has_side_effects=True, vmem_limit_bytes=56 * 1024 * 1024
        ),
        cost_estimate=pl.CostEstimate(
            flops=2 * rows * depth * 3 * attn, bytes_accessed=5 << 20, transcendentals=rows * 4096
        ),
    )(cov_slot.reshape(1, cov), block_links.T, tokens, qkv_weight, cov_embed)


def solution(mesh):
    placed = (P(("grp", "seq"), None), P(), P(("grp", "seq"), None), P(), P(("grp", "seq"), None))
    grid_shape = (mesh.shape["grp"], mesh.shape["seq"])
    return jax.shard_map(
        functools.partial(local, grid_shape),
        mesh=mesh,
        in_specs=placed,
        out_specs=P(("grp", "seq"), None),
        check_vma=False,
    )
```

```python
import functools
import math

import jax
import jax.numpy as jnp
from jax import lax
from jax.experimental import pallas as pl
from jax.experimental.pallas import tpu as pltpu
from jax.sharding import PartitionSpec as P

HEADS = 8
BLOCK = 128
LANES = 128
NT = (((1,), (1,)), ((), ()))
NN = (((1,), (0,)), ((), ()))
F32 = jnp.float32
BF16 = jnp.bfloat16
CLOSED = 1e30


def dot(a, b, dims=NN):
    return lax.dot_general(a, b, dims, preferred_element_type=F32)


def kernel(
    grid_shape,
    slot_ref,
    links_ref,
    x_hbm,
    w_hbm,
    cov_ref,
    out_ref,
    x,
    w,
    q,
    keys,
    values,
    cov_tmp,
    cov_mine,
    cov_all,
    cov_sum,
    load_sem,
    cov_send,
    cov_recv,
    halo_send,
    halo_recv,
):
    groups, seqs = grid_shape
    count = groups * seqs
    rows, depth = x.shape
    attn = q.shape[1]
    blocks = rows // BLOCK
    slots_dev = cov_ref.shape[0]
    pieces = depth // LANES
    tile_rows = slots_dev * pieces
    chosen_rows = slot_ref.shape[1]
    me = lax.axis_index("grp") * seqs + lax.axis_index("seq")

    def place(index):
        return (index // seqs, index % seqs)

    loads = [pltpu.make_async_copy(x_hbm, x, load_sem.at[0])]
    parts = 4
    step_rows = depth // parts
    for i in range(parts):
        part = pl.ds(i * step_rows, step_rows)
        loads.append(pltpu.make_async_copy(w_hbm.at[part], w.at[part], load_sem.at[i + 1]))
    for cp in loads:
        cp.start()

    barrier = pltpu.get_barrier_semaphore()

    @pl.loop(1, count)
    def _(step):
        pl.semaphore_signal(
            barrier,
            inc=1,
            device_id=place(lax.rem(me + step, count)),
            device_id_type=pl.DeviceIdType.MESH,
        )

    cov_value = cov_ref[...].astype(F32)
    for j in range(pieces):
        cov_tmp[j * slots_dev : (j + 1) * slots_dev, :] = cov_value[:, j * LANES : (j + 1) * LANES]
    cov_mine[...] = cov_tmp[...].astype(BF16)
    cov_all[me] = cov_mine[...]
    pl.semaphore_wait(barrier, count - 1)

    @pl.loop(1, count)
    def _(step):
        pltpu.make_async_remote_copy(
            src_ref=cov_mine,
            dst_ref=cov_all.at[me],
            send_sem=cov_send,
            recv_sem=cov_recv,
            device_id=place(lax.rem(me + step, count)),
            device_id_type=pl.DeviceIdType.MESH,
        ).start()

    for cp in loads:
        cp.wait()
    part = dot(x[...], w[:, attn:]).astype(BF16)
    keys[BLOCK : BLOCK + rows, :] = part[:, :attn]
    for b in range(blocks):
        values[b + 1] = part[b * BLOCK : (b + 1) * BLOCK, attn:].T

    def key_rows(b):
        return keys.at[pl.ds(b * BLOCK, BLOCK)]

    def edge_copies(source, target, peer, at):
        return [
            pltpu.make_async_remote_copy(
                src_ref=src,
                dst_ref=dst,
                send_sem=halo_send.at[at + n],
                recv_sem=halo_recv.at[at + n],
                device_id=place(peer),
                device_id_type=pl.DeviceIdType.MESH,
            )
            for n, (src, dst) in enumerate(
                [
                    (key_rows(source), key_rows(target)),
                    (values.at[source], values.at[target]),
                ]
            )
        ]

    to_left = edge_copies(1, blocks + 1, lax.max(me - 1, 0), 0)
    to_right = edge_copies(blocks, 0, lax.min(me + 1, count - 1), 2)
    has_left = me > 0
    has_right = me < count - 1

    @pl.when(has_left)
    def _():
        for cp in to_left:
            cp.start()

    @pl.when(has_right)
    def _():
        for cp in to_right:
            cp.start()

    @pl.when(me == 0)
    def _():
        keys[0:BLOCK, :] = jnp.zeros((BLOCK, attn), BF16)
        values[0] = jnp.zeros((attn, BLOCK), BF16)

    @pl.when(me == count - 1)
    def _():
        keys[BLOCK + rows : 2 * BLOCK + rows, :] = jnp.zeros((BLOCK, attn), BF16)
        values[blocks + 1] = jnp.zeros((attn, BLOCK), BF16)

    q[...] = dot(x[...], w[:, :attn]).astype(BF16)

    others = cov_all.at[pl.ds(0, count - 1)]
    pltpu.make_async_copy(others, others, cov_recv).wait()
    span = 32 if count % 32 == 0 else count
    cov_sum[...] = jnp.zeros_like(cov_sum)

    @pl.loop(0, count // span)
    def _(t):
        held = cov_all[pl.ds(t * span, span)].reshape(span * tile_rows, LANES)
        slot = slot_ref[...]
        base = (slot // slots_dev - t * span) * tile_rows + slot % slots_dev
        row = lax.broadcasted_iota(jnp.int32, (span * tile_rows, chosen_rows), 0)
        for j in range(pieces):
            pick = jnp.where(row == base + j * slots_dev, 1.0, 0.0).astype(BF16)
            cov_sum[:, j * LANES : (j + 1) * LANES] += lax.dot_general(
                pick, held, (((0,), (0,)), ((), ())), preferred_element_type=F32
            )

    chosen = cov_sum[...].astype(BF16)
    cov_keys = dot(chosen, w[:, attn : 2 * attn]).astype(BF16)
    cov_values = dot(chosen, w[:, 2 * attn :]).astype(BF16).T

    factor = math.log2(math.e) / math.sqrt(attn // HEADS)
    lane = lax.broadcasted_iota(jnp.int32, (BLOCK, LANES), 1)
    low = lane < LANES // 2

    def attend(b, p):
        cols = slice(p * LANES, (p + 1) * LANES)
        qp = q[b * BLOCK : (b + 1) * BLOCK, cols]
        zero = jnp.zeros_like(qp)
        both = jnp.concatenate([jnp.where(low, qp, zero), jnp.where(low, zero, qp)], axis=0)
        scores = dot(keys[b * BLOCK : (b + 3) * BLOCK, cols], both, NT)
        score_cov = dot(cov_keys[:, cols], both, NT)
        before, middle, after = (scores[i * BLOCK : (i + 1) * BLOCK] for i in range(3))
        open_before = links_ref[0, b] > 0
        open_after = links_ref[1, b] > 0

        def top(s):
            return jnp.max(s, axis=0, keepdims=True)

        highest = jnp.maximum(
            jnp.maximum(top(middle), top(score_cov)),
            jnp.maximum(
                jnp.where(open_before, top(before), -CLOSED),
                jnp.where(open_after, top(after), -CLOSED),
            ),
        )
        weights = [
            jnp.exp2((before - jnp.where(open_before, highest, CLOSED)) * factor),
            jnp.exp2((middle - highest) * factor),
            jnp.exp2((after - jnp.where(open_after, highest, CLOSED)) * factor),
            jnp.exp2((score_cov - highest) * factor),
        ]
        total = sum(jnp.sum(a, axis=0, keepdims=True) for a in weights)
        rounded = jnp.concatenate([a.astype(BF16) for a in weights], axis=0)
        value = jnp.concatenate(
            [values[b, cols], values[b + 1, cols], values[b + 2, cols], cov_values[cols, :]],
            axis=1,
        )
        summed = dot(value, rounded) * (1.0 / total)
        half = LANES // 2
        pair = jnp.concatenate([summed[:half, :BLOCK], summed[half:, BLOCK:]], axis=0)
        out_ref[b * BLOCK : (b + 1) * BLOCK, cols] = pair.T.astype(BF16)

    for b in range(1, blocks - 1):
        for p in range(attn // LANES):
            attend(b, p)

    @pl.when(has_left)
    def _():
        for cp in to_right:
            cp.wait_recv()

    @pl.when(has_right)
    def _():
        for cp in to_left:
            cp.wait_recv()

    for b in (0, blocks - 1):
        for p in range(attn // LANES):
            attend(b, p)

    @pl.when(has_left)
    def _():
        for cp in to_left:
            cp.wait_send()

    @pl.when(has_right)
    def _():
        for cp in to_right:
            cp.wait_send()

    pltpu.make_async_copy(others, others, cov_send).wait()


def local(grid_shape, tokens, qkv_weight, cov_embed, cov_slot, block_links):
    count = grid_shape[0] * grid_shape[1]
    rows, depth = tokens.shape
    attn = qkv_weight.shape[1] // 3
    blocks = rows // BLOCK
    tile_rows = cov_embed.shape[0] * depth // LANES
    cov = cov_slot.shape[0]
    vmem = pl.BlockSpec(memory_space=pltpu.VMEM)
    smem = pl.BlockSpec(memory_space=pltpu.SMEM)
    hbm = pl.BlockSpec(memory_space=pl.ANY)
    return pl.pallas_call(
        functools.partial(kernel, grid_shape),
        out_shape=pltpu.VMEM((rows, attn), BF16),
        in_specs=[vmem, smem, hbm, hbm, vmem],
        out_specs=vmem,
        scratch_shapes=[
            pltpu.VMEM((rows, depth), BF16),
            pltpu.VMEM((depth, 3 * attn), BF16),
            pltpu.VMEM((rows, attn), BF16),
            pltpu.VMEM((rows + 2 * BLOCK, attn), BF16),
            pltpu.VMEM((blocks + 2, attn, BLOCK), BF16),
            pltpu.VMEM((tile_rows, LANES), F32),
            pltpu.VMEM((tile_rows, LANES), BF16),
            pltpu.VMEM((count, tile_rows, LANES), BF16),
            pltpu.VMEM((cov, depth), F32),
            pltpu.SemaphoreType.DMA((7,)),
            pltpu.SemaphoreType.DMA,
            pltpu.SemaphoreType.DMA,
            pltpu.SemaphoreType.DMA((4,)),
            pltpu.SemaphoreType.DMA((4,)),
        ],
        compiler_params=pltpu.CompilerParams(
            collective_id=0, has_side_effects=True, vmem_limit_bytes=56 * 1024 * 1024
        ),
        cost_estimate=pl.CostEstimate(
            flops=2 * rows * depth * 3 * attn, bytes_accessed=5 << 20, transcendentals=rows * 4096
        ),
    )(cov_slot.reshape(1, cov), block_links.T, tokens, qkv_weight, cov_embed)


def solution(mesh):
    placed = (P(("grp", "seq"), None), P(), P(("grp", "seq"), None), P(), P(("grp", "seq"), None))
    grid_shape = (mesh.shape["grp"], mesh.shape["seq"])
    return jax.shard_map(
        functools.partial(local, grid_shape),
        mesh=mesh,
        in_specs=placed,
        out_specs=P(("grp", "seq"), None),
        check_vma=False,
    )
```
